512 devices in a mesh: dp: 64 (over y, z), mp: 8 (over x, core).
Axes of the slice: x: 4, y: 4, z: 16, core: 2. Of those that a mesh axis runs over, the one named last changes fastest.
Arguments:
- picks: int32 [64, 16], P('dp'), may hold values from 0 to 511, as said below
- query_embed: bfloat16 [64, 768], P('dp')
- dec_queries: bfloat16 [64, 8, 2048], P('dp')
- passage_states: bfloat16 [512, 32, 4096], P('dp', None, 'mp'), may hold values from -6 to 6
- retr_states: bfloat16 [512, 32, 768], P('dp', 'mp'), may hold values from -6 to 6
- key_weight: bfloat16 [4096, 2048], P(None, 'mp'), may hold values from -0.09375 to 0.09375
- retr_weight: bfloat16 [768, 768], replicated, may hold values from -0.21875 to 0.21875
Outputs:
- grad_embed: float32 [512, 768], P('dp')
- grad_query: float32 [64, 768], P('dp')
The draws below stay inside these ranges and needn't reach their ends.
Inputs may be any that keep to these rules, and one draw needn't show every extreme that they name: `picks`: the owner shard of passage id p is p // 8. Among the 16 ids of the queries of one index of dp, at most 2 lie on any one owner shard, repeats counted, and some owner shard holds exactly 2 of them for every index of dp. Some owner shards are picked far more often than others.
All inputs are finite; a program needn't handle non-finite values.
Results may differ from the reference program's by a relative error of at most 0.007.
Values may be sent and summed in bfloat16 or wider, within the bound.
A program may use at most 64 MiB of HBM per device.

```python
import jax
import jax.numpy as jnp
from jax import lax

D = 4096
HEADS = 32
HD = 64
DR = 768
L = 32
A = 8
K = 16
Q_DEV = 1
P_DEV = 8
QUERIES = 64
NPASS = 512


def draw_picks(key, part):
    key = jax.random.fold_in(key, 31)
    groups = QUERIES // Q_DEV
    owners = NPASS // P_DEV
    per_group = Q_DEV * K
    shared_heat = jax.random.randint(jax.random.fold_in(key, 11), (owners,), 0, 4)

    def one_group(group_key):
        key_order, key_heat, key_forced, key_local = jax.random.split(group_key, 4)
        order = jax.random.permutation(key_order, 2 * owners).astype(jnp.int32)
        heat = shared_heat + jax.random.randint(key_heat, (owners,), 0, 3)
        forced = jax.random.randint(key_forced, (), 0, owners)
        heat = jnp.where(jnp.arange(owners) == forced, 20, heat)
        owner_of_slot = jnp.arange(2 * owners, dtype=jnp.int32) // 2
        score = jnp.take(heat, owner_of_slot) * (2 * owners) + order
        chosen = lax.top_k(score, per_group)[1].astype(jnp.int32)
        owner_ids = chosen // 2
        local_ids = jax.random.randint(key_local, (per_group,), 0, P_DEV)
        return (owner_ids * P_DEV + local_ids).reshape(Q_DEV, K)
    group_keys = jax.random.split(jax.random.fold_in(key, 5), groups)
    return jax.vmap(one_group)(group_keys).reshape(QUERIES, K).astype(jnp.int32)


def draw_query_embed(key, part):
    key = jax.random.fold_in(key, 21)
    base = jax.random.normal(key, (QUERIES, DR), jnp.float32)
    return base.astype(jnp.bfloat16)


def draw_dec_queries(key, part):
    key = jax.random.fold_in(key, 22)
    base = jax.random.normal(key, (QUERIES, A, HEADS * HD), jnp.float32)
    return base.astype(jnp.bfloat16)


def steps_of(own_key, shape, cuts, low, top_value):
    factor_of = 1.0
    for axis_at, shards_of in cuts:
        steps = jax.random.uniform(jax.random.fold_in(jax.random.fold_in(own_key, 6), axis_at), (shards_of,), jnp.float32, low / len(cuts), top_value / len(cuts))
        factor_of = factor_of * jnp.repeat(jnp.exp(steps), shape[axis_at] // shards_of).reshape((-1,) + (1,) * (len(shape) - 1 - axis_at))
    return factor_of


def gaussian(key, dims, scale, bound, cuts=(), kind=jnp.bfloat16):
    level = steps_of(key, dims, cuts, -0.22, 0.18) if cuts else 1.0
    result = jax.random.normal(key, dims, jnp.float32) * scale * level
    return jnp.minimum(jnp.maximum(result, -bound), bound).astype(kind)


def setup_inputs(seed: int = 0) -> dict:
    key_list = jax.random.split(jax.random.key(seed), 8)
    picks = draw_picks(jax.random.fold_in(key_list[7], 71), 0)
    query_embed = draw_query_embed(jax.random.fold_in(key_list[7], 71), 0)
    dec_queries = draw_dec_queries(jax.random.fold_in(key_list[7], 71), 0)
    passage_states = gaussian(key_list[3], (NPASS, L, D), 1.0, 6.0, ((0, 64), (2, 8)))
    retr_states = gaussian(key_list[4], (NPASS, L, DR), 1.0, 6.0, ((0, 64), (1, 8)))
    key_weight = gaussian(key_list[5], (D, HEADS * HD), D ** -0.5, 0.09375, ((1, 8),))
    retr_weight = gaussian(key_list[6], (DR, DR), DR ** -0.5, 0.21875)
    return {"picks": picks, "query_embed": query_embed, "dec_queries": dec_queries, "passage_states": passage_states, "retr_states": retr_states, "key_weight": key_weight, "retr_weight": retr_weight}


def reference(picks, query_embed, dec_queries, passage_states, retr_states, key_weight, retr_weight):
    weight_full = key_weight.astype(jnp.float32).reshape(D, HEADS, HD)

    def one_query(items):
        ids, query, decoder = items
        states = jnp.take(passage_states, ids, axis=0).astype(jnp.float32).reshape(K * L, D)
        dec_full = decoder.astype(jnp.float32).reshape(A, HEADS, HD)
        probes = jnp.einsum("whd,ahd->ahw", weight_full, dec_full, precision=lax.Precision.HIGHEST)
        scores = jnp.einsum("sw,ahw->ahs", states, probes, precision=lax.Precision.HIGHEST)
        attn = jax.nn.softmax(scores, axis=-1)
        mass = jnp.sum(attn.reshape(A, HEADS, K, L), axis=(0, 1, 3)) / (A * HEADS)
        tokens = jnp.take(retr_states, ids, axis=0).astype(jnp.float32)
        pooled = (jnp.sum(tokens, axis=1) / L).astype(jnp.bfloat16)
        embeds = jnp.dot(pooled, retr_weight, preferred_element_type=jnp.float32)
        query_full = query.astype(jnp.float32)
        retr_scores = jnp.einsum("kr,r->k", embeds, query_full, precision=lax.Precision.HIGHEST)
        retr_probs = jax.nn.softmax(retr_scores, axis=-1)
        delta = retr_probs - mass
        grad_q = jnp.einsum("k,kr->r", delta, embeds, precision=lax.Precision.HIGHEST)
        grad_e = delta[:, None] * query_full[None, :]
        return grad_e, grad_q

    grad_each, grad_query = lax.map(one_query, (picks, query_embed, dec_queries))
    grad_embed = jax.ops.segment_sum(grad_each.reshape(QUERIES * K, DR), picks.reshape(QUERIES * K), num_segments=NPASS)
    return grad_embed, grad_query
```

```python
import functools

import jax
import jax.numpy as jnp
from jax import lax
from jax.experimental import pallas as pl
from jax.experimental.pallas import tpu as pltpu
from jax.sharding import PartitionSpec as P

HD = 64
MESH = pl.DeviceIdType.MESH
HIGH = lax.Precision.HIGHEST
NEG = -3e38
F32 = jnp.float32
BF16 = jnp.bfloat16
NT = (((1,), (1,)), ((), ()))
CHUNKS = 4
Y = 4
X = 4


def dot(a, b):
    return jnp.dot(a, b, preferred_element_type=F32)


def dot_nt(a, b):
    return lax.dot_general(a, b, NT, preferred_element_type=F32)


def split3(a):
    first = a.astype(BF16)
    rest = a - first.astype(F32)
    second = rest.astype(BF16)
    third = (rest - second.astype(F32)).astype(BF16)
    return first, second, third


def kernel(
    Z, length, total_heads,
    picks, qe, dec, states, retr, kw, rw,
    ge_out, gq_out,
    st, wb, wrb, gb, ym, pp, pr, pg, bt, qx, q8, c4, cm, em, r4, ob, lz, yb, mb, dz, dt, gs, gyr,
    load_sem, st_s, st_r, gz_s, gz_r, gy_s, gy_r, ym_s, ym_r, pr_s, pr_r, pg_s, pg_r, pc_s, pc_r,
    lz_s, lz_r, yb_s, yb_r, mb_s, mb_r, dz_s, dz_r, qy_s, qy_r,
):
    d = lax.axis_index("dp")
    m = lax.axis_index("mp")
    y, z = d // Z, lax.rem(d, Z)
    x, c = m // 2, lax.rem(m, 2)
    M8 = 2 * X
    other = 1 - c
    xl, xr, xo = lax.rem(x + X - 1, X), lax.rem(x + 1, X), lax.rem(x + 2, X)
    mL, mR, mO, sib = xl * 2 + c, xr * 2 + c, xo * 2 + c, x * 2 + other
    sL, sR, sO = xl * 2 + other, xr * 2 + other, xo * 2 + other
    width = states.shape[1]
    rows = states.shape[0]
    step = rows // CHUNKS
    answers = dec.shape[0]
    p_dev = rows // length
    dr = qe.shape[1]
    nb = dr // 128
    half = nb // 2

    load_st = pltpu.make_async_copy(states, st.at[m], load_sem.at[0])
    load_w = pltpu.make_async_copy(kw, wb, load_sem.at[1])
    load_r = pltpu.make_async_copy(rw, wrb, load_sem.at[2])
    load_st.start()
    load_w.start()
    load_r.start()

    barrier = pltpu.get_barrier_semaphore()

    def hello(i, carry):
        zt = lax.rem(z + i, Z)
        pl.semaphore_signal(barrier, inc=1, device_id=(y * Z + zt, m), device_id_type=MESH)
        return carry

    lax.fori_loop(1, Z, hello, 0)
    for i in range(1, Y):
        pl.semaphore_signal(barrier, inc=1, device_id=(lax.rem(y + i, Y) * Z + z, m), device_id_type=MESH)
    for i in range(1, M8):
        pl.semaphore_signal(barrier, inc=1, device_id=(d, lax.rem(m + i, M8)), device_id_type=MESH)

    part = jnp.sum(retr[...].astype(F32), axis=1)
    for h in range(2):
        for j in range(half):
            b = h * half + j
            pp[h, j * p_dev:(j + 1) * p_dev, :] = part[:, b * 128:(b + 1) * 128]

    ident = lax.broadcasted_iota(jnp.int32, (8, 128), 0) * 128 + lax.broadcasted_iota(jnp.int32, (8, 128), 1)
    counts = jnp.zeros((8, 128), F32)
    for k in range(picks.shape[1]):
        counts = counts + jnp.where(ident == picks[0, k], 1.0, 0.0)
    ym[y, 0:8, :] = jnp.zeros((8, 128), F32)
    qf = qe[...].astype(F32)
    for j in range(nb):
        ym[y, j:j + 1, :] = qf[:, j * 128:(j + 1) * 128]
    ym[y, 8:16, :] = counts

    mine = dec[:, pl.ds(pl.multiple_of(m * 256, 256), 256)].astype(F32)
    block = jnp.concatenate(
        [mine[:, :128], mine[:, 128:], ym[y, 0:8, :], jnp.zeros((8, 128), F32)], axis=0
    )
    gb[y, z] = block.astype(BF16)

    load_st.wait()
    pl.semaphore_wait(barrier, Z - 1 + Y - 1 + M8 - 1)

    def pool_copy(i):
        to = lax.rem(m + i, M8)
        return pltpu.make_async_remote_copy(
            pp.at[lax.rem(to, 2)], pr.at[m], pr_s.at[i], pr_r.at[m], device_id=(d, to), device_id_type=MESH
        )

    def pool_from(i):
        src = lax.rem(m + i, M8)
        return pltpu.make_async_remote_copy(
            pp.at[0], pr.at[src], pr_s.at[0], pr_r.at[src], device_id=(d, sib), device_id_type=MESH
        )

    def block_copy(src, j, to, k):
        at = st.at[src, pl.ds(j * step, step), :]
        return pltpu.make_async_remote_copy(
            at, at, st_s.at[k], st_r.at[src, j], device_id=(d, to), device_id_type=MESH
        )

    def gz_copy(i):
        zt = lax.rem(z + i, Z)
        return pltpu.make_async_remote_copy(
            gb.at[y, z], gb.at[y, z], gz_s.at[i], gz_r.at[z], device_id=(y * Z + zt, m), device_id_type=MESH
        )

    def gz_from(i):
        src = lax.rem(z + i, Z)
        return pltpu.make_async_remote_copy(
            gb.at[y, src], gb.at[y, src], gz_s.at[0], gz_r.at[src], device_id=(y * Z + src, m), device_id_type=MESH
        )

    def y_copy(buf, ssem, rsem, i):
        to = lax.rem(y + i, Y) * Z + z
        return pltpu.make_async_remote_copy(
            buf.at[y], buf.at[y], ssem.at[i], rsem.at[y], device_id=(to, m), device_id_type=MESH
        )

    def y_from(buf, ssem, rsem, i):
        src = lax.rem(y + i, Y)
        return pltpu.make_async_remote_copy(
            buf.at[src], buf.at[src], ssem.at[0], rsem.at[src], device_id=(src * Z + z, m), device_id_type=MESH
        )

    def pg_copy(i):
        zt = lax.rem(z + i, Z)
        return pltpu.make_async_remote_copy(
            pg.at[c, z], pg.at[c, z], pg_s.at[i], pg_r.at[z], device_id=(y * Z + zt, m), device_id_type=MESH
        )

    def pg_from(i):
        src = lax.rem(z + i, Z)
        return pltpu.make_async_remote_copy(
            pg.at[c, src], pg.at[c, src], pg_s.at[0], pg_r.at[src], device_id=(y * Z + src, m), device_id_type=MESH
        )

    def loop(make, act):
        def one(i, carry):
            getattr(make(i), act)()
            return carry

        lax.fori_loop(1, Z, one, 0)

    sent = []

    def push(src, j, to):
        copy = block_copy(src, j, to, len(sent))
        copy.start()
        sent.append(copy)

    def arrived(src, j):
        block_copy(src, j, sib, 0).wait_recv()

    for i in range(1, M8):
        pool_copy(i).start()
    for i in range(CHUNKS):
        push(m, i, mR)
        push(m, (i + CHUNKS // 2) % CHUNKS, mL)
        push(m, i, sib)
    loop(gz_copy, "start")
    for i in range(1, Y):
        y_copy(ym, ym_s, ym_r, i).start()

    load_w.wait()

    def product(src):
        return dot(st[src], wb[pl.ds(pl.multiple_of(src * width, width), width), :])

    keys = product(m)

    for i in range(1, M8):
        pool_from(i).wait_recv()
    pooled = pp[c]
    for i in range(1, M8):
        pooled = pooled + pr[lax.rem(m + i, M8)]
    pooled = pooled / length
    pg[c, z] = jnp.concatenate([pooled, jnp.zeros((32 - half * p_dev, 128), F32)], axis=0).astype(BF16)
    loop(pg_copy, "start")

    h2 = CHUNKS // 2
    for j in range(h2):
        arrived(mL, j)
        push(mL, j, mR)
        push(mL, j, sib)
        arrived(mR, j + h2)
        push(mR, j + h2, mL)
        push(mR, j + h2, sib)

    for i in range(1, Y):
        y_from(ym, ym_s, ym_r, i).wait_recv()
    q8[...] = jnp.zeros_like(q8)
    c4[...] = jnp.zeros_like(c4)
    for i in range(Y):
        c4[i:i + 1, :] = ym[i, pl.ds(8 + y, 1), :]
        for j in range(nb):
            q8[i:i + 1, j * 128:(j + 1) * 128] = ym[i, j:j + 1, :]
    spread = jnp.concatenate(
        [jnp.broadcast_to(c4[i:i + 1, :], (answers, 128)) for _ in range(128 // (Y * answers)) for i in range(Y)], axis=0
    )
    cm[...] = spread.T

    for j in range(h2):
        arrived(mL, j + h2)
        push(mL, j + h2, sib)
        arrived(mR, j)
        push(mR, j, sib)
        if j == 0:
            loop(gz_from, "wait_recv")
            for i in range(1, Y):
                y_copy(gb, gy_s, gy_r, i).start()
    for j in range(CHUNKS):
        arrived(sib, j)
    keys = keys + product(mL) + product(mR) + product(sib)

    for j in range(h2):
        arrived(mO, j)
        push(mO, j, sib)
        arrived(mO, j + h2)
        push(mO, j + h2, sib)
    keys = keys + product(mO)

    for i in range(1, Y):
        y_from(gb, gy_s, gy_r, i).wait_recv()
    low = lax.broadcasted_iota(jnp.int32, (8, 128), 1) < HD
    zero = jnp.zeros((8, 128), F32)
    zeros = jnp.zeros((64, 128), F32)

    def spread_queries(s, carry):
        got = [gb[i, s].astype(F32) for i in range(Y)]
        left = [jnp.where(low, g[0:8], zero) for g in got] + [jnp.where(low, zero, g[0:8]) for g in got]
        right = [jnp.where(low, g[8:16], zero) for g in got] + [jnp.where(low, zero, g[8:16]) for g in got]
        left = jnp.concatenate(left + [zeros], axis=0)
        right = jnp.concatenate([zeros] + right, axis=0)
        bt[s] = jnp.concatenate([left, right], axis=1).astype(BF16)
        qx[s] = jnp.zeros((8, dr), F32)
        for i in range(Y):
            for j in range(nb):
                qx[s, i:i + 1, j * 128:(j + 1) * 128] = got[i][16 + j:17 + j, :]
        return carry

    lax.fori_loop(0, Z, spread_queries, 0)

    for src in (sL, sR, sO):
        for j in range(CHUNKS):
            arrived(src, j)
        keys = keys + product(src)

    to_row = lax.broadcasted_iota(jnp.int32, (rows, rows), 0)
    from_row = lax.broadcasted_iota(jnp.int32, (rows, rows), 1)
    perm = jnp.where(
        from_row == lax.rem(to_row, p_dev) * length + to_row // p_dev, 1.0, 0.0
    ).astype(BF16)
    k1, k2, k3 = [dot(perm, k).astype(BF16) for k in split3(keys)]

    def lz_copy(zt, k):
        return pltpu.make_async_remote_copy(
            ob.at[zt], lz.at[z], lz_s.at[k], lz_r.at[z], device_id=(y * Z + zt, m), device_id_type=MESH
        )

    def lz_from(i):
        src = lax.rem(z + i, Z)
        return pltpu.make_async_remote_copy(
            ob.at[src], lz.at[src], lz_s.at[0], lz_r.at[src], device_id=(y * Z + src, m), device_id_type=MESH
        )

    def lse_pair(z0, z1):
        both = jnp.concatenate([bt[z0], bt[z1]], axis=0)
        scores = dot_nt(k1, both) + dot_nt(k2, both) + dot_nt(k3, both)
        scores = scores.reshape(length, p_dev, 256)
        top = jnp.max(scores, axis=0)
        return top + jnp.log(jnp.sum(jnp.exp(scores - top[None]), axis=0))

    def far_near(i):
        return lax.rem(z + Z // 2 + i, Z), lax.rem(z + Z // 2 - 1 - i, Z)

    def score_step(i, carry):
        z0, z1 = far_near(i)
        lse = lse_pair(z0, z1)
        ob[z0] = lse[:, :128]
        ob[z1] = lse[:, 128:]
        lz_copy(z0, 2 * i).start()
        lz_copy(z1, 2 * i + 1).start()
        return carry

    lax.fori_loop(0, Z // 2 - 1, score_step, 0)
    zlast, _ = far_near(Z // 2 - 1)
    lse = lse_pair(zlast, z)
    ob[zlast] = lse[:, :128]
    lz_copy(zlast, Z - 2).start()
    lz[z] = lse[:, 128:]

    loop(pg_from, "wait_recv")
    core_copy = pltpu.make_async_remote_copy(
        pg.at[c], pg.at[c], pc_s, pc_r, device_id=(d, sib), device_id_type=MESH
    )
    core_copy.start()
    load_r.wait()
    pltpu.make_async_remote_copy(
        pg.at[other], pg.at[other], pc_s, pc_r, device_id=(d, sib), device_id_type=MESH
    ).wait_recv()
    embeds = None
    for h in range(2):
        got = pg[h].astype(F32)
        for j in range(half):
            b = h * half + j
            piece = got[:, j * p_dev:(j + 1) * p_dev, :].reshape(Z * p_dev, 128).astype(BF16)
            term = dot(piece, wrb[b * 128:(b + 1) * 128, :])
            embeds = term if embeds is None else embeds + term
    em[...] = embeds
    count4 = c4[...]
    rs = lax.dot_general(q8[...], embeds, NT, precision=HIGH, preferred_element_type=F32)
    rs = jnp.where(count4 > 0, rs, NEG)
    rtop = jnp.max(rs, axis=1, keepdims=True)
    rsum = jnp.sum(count4 * jnp.exp(rs - rtop), axis=1, keepdims=True)
    rlse = rtop + jnp.log(jnp.where(rsum > 0, rsum, 1.0))

    loop(lz_from, "wait_recv")
    count = cm[...]
    own = jnp.where(count > 0, lz[...].reshape(128, 128), NEG)
    top = jnp.max(own, axis=0, keepdims=True)
    total = jnp.sum(count * jnp.exp(own - top), axis=0, keepdims=True)
    alse = top + jnp.log(jnp.where(total > 0, total, 1.0))
    row = lax.broadcasted_iota(jnp.int32, (8, 128), 0)
    yb[y] = jnp.where(row == 4, jnp.broadcast_to(alse, (8, 128)), jnp.broadcast_to(rlse, (8, 128)))
    for i in range(1, Y):
        y_copy(yb, yb_s, yb_r, i).start()
    for i in range(1, Y):
        y_from(yb, yb_s, yb_r, i).wait_recv()
    parts = yb[...]
    top = jnp.max(parts, axis=0)
    whole = top + jnp.log(jnp.sum(jnp.exp(parts - top[None]), axis=0))
    attn = count * jnp.exp(own - whole[4:5, :])
    lane = lax.broadcasted_iota(jnp.int32, (8, 128), 1)
    group = jnp.where(lax.rem(lane // answers, Y) == row, 1.0, 0.0)
    mass = lax.dot_general(group, attn, NT, precision=HIGH, preferred_element_type=F32)
    mb[m] = mass / (answers * total_heads)

    def mb_copy(i):
        return pltpu.make_async_remote_copy(
            mb.at[m], mb.at[m], mb_s.at[i], mb_r.at[m], device_id=(d, lax.rem(m + i, M8)), device_id_type=MESH
        )

    def mb_from(i):
        src = lax.rem(m + i, M8)
        return pltpu.make_async_remote_copy(
            mb.at[src], mb.at[src], mb_s.at[0], mb_r.at[src], device_id=(d, src), device_id_type=MESH
        )

    for i in range(1, M8):
        mb_copy(i).start()
    probs = count4 * jnp.exp(rs - whole)
    for i in range(1, M8):
        mb_from(i).wait_recv()
    delta = probs - jnp.sum(mb[...], axis=0)
    dz[z] = delta

    def dz_copy(i):
        zt = lax.rem(z + i, Z)
        return pltpu.make_async_remote_copy(
            dz.at[z], dz.at[z], dz_s.at[i], dz_r.at[z], device_id=(y * Z + zt, m), device_id_type=MESH
        )

    def dz_from(i):
        src = lax.rem(z + i, Z)
        return pltpu.make_async_remote_copy(
            dz.at[src], dz.at[src], dz_s.at[0], dz_r.at[src], device_id=(y * Z + src, m), device_id_type=MESH
        )

    loop(dz_copy, "start")
    grads = jnp.dot(delta, em[...], precision=HIGH, preferred_element_type=F32)
    for i in range(Y):
        gs[i] = grads[i:i + 1, :]

    def qy_copy(i):
        to = lax.rem(y + i, Y)
        return pltpu.make_async_remote_copy(
            gs.at[to], gyr.at[y], qy_s.at[i], qy_r.at[y], device_id=(to * Z + z, m), device_id_type=MESH
        )

    def qy_from(i):
        src = lax.rem(y + i, Y)
        return pltpu.make_async_remote_copy(
            gs.at[src], gyr.at[src], qy_s.at[0], qy_r.at[src], device_id=(src * Z + z, m), device_id_type=MESH
        )

    for i in range(1, Y):
        qy_copy(i).start()
    gyr[y] = gs[y]
    loop(dz_from, "wait_recv")
    dt[...] = dz[...].reshape(Z * 8, 128).T
    back = dt[pl.ds(pl.multiple_of(z * p_dev, 8), p_dev), :]
    embed_all = qx[...].reshape(Z * 8, dr).astype(BF16)
    b1, b2, b3 = split3(back)
    ge_out[...] = dot(b1, embed_all) + dot(b2, embed_all) + dot(b3, embed_all)
    for i in range(1, Y):
        qy_from(i).wait_recv()
    gq_out[...] = gyr[0] + gyr[1] + gyr[2] + gyr[3]

    for copy in sent:
        copy.wait_send()
    for i in range(1, M8):
        pool_copy(i).wait_send()
        mb_copy(i).wait_send()
    for i in range(1, Y):
        y_copy(ym, ym_s, ym_r, i).wait_send()
        y_copy(gb, gy_s, gy_r, i).wait_send()
        y_copy(yb, yb_s, yb_r, i).wait_send()
        qy_copy(i).wait_send()
    core_copy.wait_send()

    def sent_one(i, carry):
        gz_copy(i).wait_send()
        pg_copy(i).wait_send()
        dz_copy(i).wait_send()
        lz_copy(0, i - 1).wait_send()
        return carry

    lax.fori_loop(1, Z, sent_one, 0)


def body(picks, query_embed, dec_queries, passage_states, retr_states, key_weight, retr_weight):
    dp = lax.axis_size("dp")
    mp = lax.axis_size("mp")
    Z = dp // Y
    p_dev, length, width = passage_states.shape
    answers, all_cols = dec_queries.shape[1:]
    dr = retr_weight.shape[0]
    rows = p_dev * length
    states = passage_states.reshape(rows, width)
    dec = dec_queries.reshape(answers, all_cols)
    half_rows = (dr // 256) * p_dev
    dma = pltpu.SemaphoreType.DMA
    vmem = pl.BlockSpec(memory_space=pltpu.VMEM)
    hbm = pl.BlockSpec(memory_space=pl.ANY)
    ge, gq = pl.pallas_call(
        functools.partial(kernel, Z, length, all_cols // HD),
        out_shape=(
            jax.ShapeDtypeStruct((p_dev, dr), F32),
            jax.ShapeDtypeStruct((1, dr), F32),
        ),
        in_specs=[pl.BlockSpec(memory_space=pltpu.SMEM), vmem, vmem, hbm, vmem, hbm, hbm],
        out_specs=(vmem, vmem),
        scratch_shapes=[
            pltpu.VMEM((mp, rows, width), BF16),
            pltpu.VMEM(key_weight.shape, BF16),
            pltpu.VMEM((dr, dr), BF16),
            pltpu.VMEM((Y, Z, 32, 128), BF16),
            pltpu.VMEM((Y, 16, 128), F32),
            pltpu.VMEM((2, half_rows, 128), F32),
            pltpu.VMEM((mp, half_rows, 128), F32),
            pltpu.VMEM((2, Z, 32, 128), BF16),
            pltpu.VMEM((Z, 128, 256), BF16),
            pltpu.VMEM((Z, 8, dr), F32),
            pltpu.VMEM((8, dr), F32),
            pltpu.VMEM((8, 128), F32),
            pltpu.VMEM((128, 128), F32),
            pltpu.VMEM((128, dr), F32),
            pltpu.VMEM((8, 128), F32),
            pltpu.VMEM((Z, 8, 128), F32),
            pltpu.VMEM((Z, 8, 128), F32),
            pltpu.VMEM((Y, 8, 128), F32),
            pltpu.VMEM((mp, 8, 128), F32),
            pltpu.VMEM((Z, 8, 128), F32),
            pltpu.VMEM((128, 128), F32),
            pltpu.VMEM((Y, 1, dr), F32),
            pltpu.VMEM((Y, 1, dr), F32),
            dma((3,)),
            dma((28,)), dma((mp, CHUNKS)),
            dma((Z,)), dma((Z,)),
            dma((Y,)), dma((Y,)),
            dma((Y,)), dma((Y,)),
            dma((mp,)), dma((mp,)),
            dma((Z,)), dma((Z,)),
            dma, dma,
            dma((Z,)), dma((Z,)),
            dma((Y,)), dma((Y,)),
            dma((mp,)), dma((mp,)),
            dma((Z,)), dma((Z,)),
            dma((Y,)), dma((Y,)),
        ],
        compiler_params=pltpu.CompilerParams(
            collective_id=0, has_side_effects=True, vmem_limit_bytes=40 * 1024 * 1024
        ),
    )(picks, query_embed, dec, states, retr_states, key_weight, retr_weight)
    return ge, gq


def solution(mesh):
    placed = (
        P("dp", None),
        P("dp", None),
        P("dp", None, None),
        P("dp", None, "mp"),
        P("dp", "mp", None),
        P(None, "mp"),
        P(),
    )
    return jax.shard_map(
        body, mesh=mesh, in_specs=placed, out_specs=(P("dp", None), P("dp", None)), check_vma=False
    )
```

```python
import functools

import jax
import jax.numpy as jnp
from jax import lax
from jax.experimental import pallas as pl
from jax.experimental.pallas import tpu as pltpu
from jax.sharding import PartitionSpec as P

HD = 64
MESH = pl.DeviceIdType.MESH
NEG = -3e38
F32 = jnp.float32
BF16 = jnp.bfloat16
NT = (((1,), (1,)), ((), ()))
CHUNKS = 4
Y = 4
X = 4


def dot(a, b):
    return jnp.dot(a, b, preferred_element_type=F32)


def dot_nt(a, b):
    return lax.dot_general(a, b, NT, preferred_element_type=F32)


def split2(a):
    first = a.astype(BF16)
    return first, (a - first.astype(F32)).astype(BF16)


def kernel(
    Z, length, total_heads,
    picks_hbm, qe_hbm, dec_hbm, states, retr_hbm, kw, rw,
    ge_out, gq_out,
    picks, qe, dec, retr, st, wb, wrb, gb, qb, ym, pp, pr, pg, qx, q8, c4, cm, em, ob, lz, yb, mb, dz, gs, gyr,
    load_sem, st_s, st_r, gz_s, gz_r, gy_s, gy_r, qz_s, qz_r, qw_s, qw_r, ym_s, ym_r, pr_s, pr_r, pg_s, pg_r,
    pc_s, pc_r, lz_s, lz_r, yb_s, yb_r, mb_s, mb_r, dz_s, dz_r, qy_s, qy_r,
):
    d = lax.axis_index("dp")
    m = lax.axis_index("mp")
    y, z = d // Z, lax.rem(d, Z)
    x, c = m // 2, lax.rem(m, 2)
    M8 = 2 * X
    other = 1 - c
    xl, xr, xo = lax.rem(x + X - 1, X), lax.rem(x + 1, X), lax.rem(x + 2, X)
    mL, mR, mO, sib = xl * 2 + c, xr * 2 + c, xo * 2 + c, x * 2 + other
    sL, sR, sO = xl * 2 + other, xr * 2 + other, xo * 2 + other
    rows, width = states.shape
    step = rows // CHUNKS
    answers = dec.shape[0]
    p_dev = rows // length
    dr = qe.shape[1]
    nb = dr // 128
    half = nb // 2

    load_st = pltpu.make_async_copy(states, st.at[m], load_sem.at[0])
    load_w = pltpu.make_async_copy(kw, wb, load_sem.at[1])
    load_r = pltpu.make_async_copy(rw, wrb, load_sem.at[2])
    load_dec = pltpu.make_async_copy(dec_hbm, dec, load_sem.at[3])
    load_qe = pltpu.make_async_copy(qe_hbm, qe, load_sem.at[4])
    load_picks = pltpu.make_async_copy(picks_hbm, picks, load_sem.at[5])
    load_retr = pltpu.make_async_copy(retr_hbm, retr, load_sem.at[6])
    for copy in (load_dec, load_qe, load_picks, load_retr, load_st, load_w, load_r):
        copy.start()

    barrier = pltpu.get_barrier_semaphore()

    def hello(i, carry):
        zt = lax.rem(z + i, Z)
        pl.semaphore_signal(barrier, inc=1, device_id=(y * Z + zt, m), device_id_type=MESH)
        return carry

    lax.fori_loop(1, Z, hello, 0)
    for i in range(1, Y):
        pl.semaphore_signal(barrier, inc=1, device_id=(lax.rem(y + i, Y) * Z + z, m), device_id_type=MESH)
    for i in range(1, M8):
        pl.semaphore_signal(barrier, inc=1, device_id=(d, lax.rem(m + i, M8)), device_id_type=MESH)

    pl.semaphore_wait(barrier, Z - 1 + Y - 1 + M8 - 1)
    def remote(src, dst, ssem, rsem, dev):
        return pltpu.make_async_remote_copy(src, dst, ssem, rsem, device_id=dev, device_id_type=MESH)

    def z_send(buf, ssem, rsem):
        def one(i, carry):
            zt = lax.rem(z + i, Z)
            remote(buf.at[z], buf.at[z], ssem, rsem, (y * Z + zt, m)).start()
            return carry

        lax.fori_loop(1, Z, one, 0)

    def z_all(buf, ssem, rsem):
        at = buf.at[pl.ds(0, Z - 1)]
        return remote(at, at, ssem, rsem, (y * Z + lax.rem(z + 1, Z), m))

    def y_copy(buf, ssem, rsem, i):
        to = lax.rem(y + i, Y) * Z + z
        return remote(buf.at[y], buf.at[y], ssem, rsem, (to, m))

    def y_all(buf, ssem, rsem):
        at = buf.at[pl.ds(0, Y - 1)]
        return remote(at, at, ssem, rsem, (lax.rem(y + 1, Y) * Z + z, m))

    def y_send(buf, ssem, rsem):
        for i in range(1, Y):
            y_copy(buf, ssem, rsem, i).start()

    sent = []

    def push(src, j, to, own=False):
        k = len(sent)
        at = st.at[src, pl.ds(j * step, step), :]
        copy = remote(states.at[pl.ds(j * step, step), :] if own else at, at, st_s.at[k], st_r.at[src, j], (d, to))
        copy.start()
        sent.append(copy)

    def arrived(src, j):
        at = st.at[src, pl.ds(j * step, step), :]
        remote(at, at, st_s.at[0], st_r.at[src, j], (d, sib)).wait_recv()

    gz = gb.at[y]
    h2 = CHUNKS // 2
    for i in range(h2):
        push(m, i, mR, True)
        push(m, i + h2, mL, True)

    load_dec.wait()
    mine = dec[:, pl.ds(pl.multiple_of(m * 256, 256), 256)].astype(F32)
    gb[y, z] = jnp.concatenate([mine[:, :128], mine[:, 128:]], axis=0).astype(BF16)
    z_send(gz, gz_s, gz_r)

    load_retr.wait()
    part = jnp.sum(retr[...].astype(F32), axis=1)
    for h in range(2):
        for j in range(half):
            b = h * half + j
            pp[h, j * p_dev:(j + 1) * p_dev, :] = part[:, b * 128:(b + 1) * 128]

    def pool_copy(i):
        to = lax.rem(m + i, M8)
        return remote(pp.at[lax.rem(to, 2)], pr.at[m], pr_s, pr_r, (d, to))

    for i in range(1, M8):
        pool_copy(i).start()

    for i in range(h2):
        push(m, i + h2, mR, True)
        push(m, i, mL, True)
    for i in range(CHUNKS):
        push(m, i, sib, True)

    load_picks.wait()
    load_qe.wait()
    ident = lax.broadcasted_iota(jnp.int32, (8, 128), 0) * 128 + lax.broadcasted_iota(jnp.int32, (8, 128), 1)
    counts = jnp.zeros((8, 128), F32)
    for k in range(picks.shape[1]):
        counts = counts + jnp.where(ident == picks[0, k], 1.0, 0.0)
    ym[y, 0:8, :] = jnp.zeros((8, 128), F32)
    qf = qe[...].astype(F32)
    for j in range(nb):
        ym[y, j:j + 1, :] = qf[:, j * 128:(j + 1) * 128]
    ym[y, 8:16, :] = counts
    qb[y, z] = ym[y, 0:8, :]
    y_send(ym, ym_s, ym_r)
    z_send(qb.at[y], qz_s, qz_r)

    load_st.wait()
    load_w.wait()

    def product(src):
        return dot(st[src], wb[pl.ds(pl.multiple_of(src * width, width), width), :])

    keys = product(m)

    for j in range(h2):
        arrived(mL, j)
        push(mL, j, mR)
        push(mL, j, sib)
        arrived(mR, j + h2)
        push(mR, j + h2, mL)
        push(mR, j + h2, sib)

    pool_all = remote(pr.at[pl.ds(0, M8 - 1)], pr.at[pl.ds(0, M8 - 1)], pr_s, pr_r, (d, sib))
    pool_all.wait_recv()
    pooled = pp[c]
    for i in range(1, M8):
        pooled = pooled + pr[lax.rem(m + i, M8)]
    pooled = pooled / length
    pg[c, z] = jnp.concatenate([pooled, jnp.zeros((32 - half * p_dev, 128), F32)], axis=0).astype(BF16)
    z_send(pg.at[c], pg_s, pg_r)

    for j in range(h2):
        arrived(mL, j + h2)
        push(mL, j + h2, sib)
        arrived(mR, j)
        push(mR, j, sib)

    z_all(gz, gz_s, gz_r).wait_recv()
    y_send(gb, gy_s, gy_r)

    y_all(ym, ym_s, ym_r).wait_recv()
    q8[...] = jnp.zeros_like(q8)
    c4[...] = jnp.zeros_like(c4)
    for i in range(Y):
        c4[i:i + 1, :] = ym[i, pl.ds(8 + y, 1), :]
        for j in range(nb):
            q8[i:i + 1, j * 128:(j + 1) * 128] = ym[i, j:j + 1, :]
    spread = jnp.concatenate(
        [jnp.broadcast_to(c4[i:i + 1, :], (answers, 128)) for _ in range(128 // (Y * answers)) for i in range(Y)], axis=0
    )
    cm[...] = spread.T

    for j in range(CHUNKS):
        arrived(sib, j)
    keys = keys + product(mL) + product(mR) + product(sib)
    for j in range(h2):
        arrived(mO, j)
        push(mO, j, sib)
        arrived(mO, j + h2)
        push(mO, j + h2, sib)
    keys = keys + product(mO)
    for src in (sL, sR, sO):
        for j in range(CHUNKS):
            arrived(src, j)
        keys = keys + product(src)

    to_row = lax.broadcasted_iota(jnp.int32, (rows, rows), 0)
    from_row = lax.broadcasted_iota(jnp.int32, (rows, rows), 1)
    perm = jnp.where(
        from_row == lax.rem(to_row, p_dev) * length + to_row // p_dev, 1.0, 0.0
    ).astype(BF16)
    k1, k2 = [dot(perm, k).astype(BF16) for k in split2(keys)]

    y_all(gb, gy_s, gy_r).wait_recv()
    low = lax.broadcasted_iota(jnp.int32, (8, 128), 1) < HD
    zero = jnp.zeros((8, 128), F32)
    zeros = jnp.zeros((64, 128), F32)

    def spread_queries(s):
        got = [gb[i, s].astype(F32) for i in range(Y)]
        left = [jnp.where(low, g[0:8], zero) for g in got] + [jnp.where(low, zero, g[0:8]) for g in got]
        right = [jnp.where(low, g[8:16], zero) for g in got] + [jnp.where(low, zero, g[8:16]) for g in got]
        left = jnp.concatenate(left + [zeros], axis=0)
        right = jnp.concatenate([zeros] + right, axis=0)
        return jnp.concatenate([left, right], axis=1).astype(BF16)

    def lz_copy(zt):
        return remote(ob.at[zt], lz.at[z], lz_s, lz_r, (y * Z + zt, m))

    def lse_pair(z0, z1):
        both = jnp.concatenate([spread_queries(z0), spread_queries(z1)], axis=0)
        scores = dot_nt(k1, both) + dot_nt(k2, both)
        scores = scores.reshape(length, p_dev, 256)
        top = jnp.max(scores, axis=0)
        return top + jnp.log(jnp.sum(jnp.exp(scores - top[None]), axis=0))

    def far_near(i):
        return lax.rem(z + Z // 2 + i, Z), lax.rem(z + Z // 2 - 1 - i, Z)

    def score_step(i, carry):
        z0, z1 = far_near(i)
        lse = lse_pair(z0, z1)
        ob[z0] = lse[:, :128]
        ob[z1] = lse[:, 128:]
        lz_copy(z0).start()
        lz_copy(z1).start()
        return carry

    lax.fori_loop(0, Z // 2 - 1, score_step, 0)
    zlast, _ = far_near(Z // 2 - 1)
    lse = lse_pair(zlast, z)
    ob[zlast] = lse[:, :128]
    lz_copy(zlast).start()
    lz[z] = lse[:, 128:]

    z_all(qb.at[y], qz_s, qz_r).wait_recv()
    y_send(qb, qw_s, qw_r)

    pgz = pg.at[c]
    z_all(pgz, pg_s, pg_r).wait_recv()
    core_copy = remote(pg.at[c], pg.at[c], pc_s, pc_r, (d, sib))
    core_copy.start()
    load_r.wait()
    remote(pg.at[other], pg.at[other], pc_s, pc_r, (d, sib)).wait_recv()
    embeds = None
    for h in range(2):
        got = pg[h].astype(F32)
        for j in range(half):
            b = h * half + j
            piece = got[:, j * p_dev:(j + 1) * p_dev, :].reshape(Z * p_dev, 128).astype(BF16)
            term = dot(piece, wrb[b * 128:(b + 1) * 128, :])
            embeds = term if embeds is None else embeds + term
    e1, e2 = split2(embeds)
    em[0] = e1
    em[1] = e2
    count4 = c4[...]
    q1 = q8[...].astype(BF16)
    rs = dot_nt(q1, e1) + dot_nt(q1, e2) + dot_nt(q1, (embeds - e1.astype(F32) - e2.astype(F32)).astype(BF16))
    rs = jnp.where(count4 > 0, rs, NEG)
    rtop = jnp.max(rs, axis=1, keepdims=True)
    rsum = jnp.sum(count4 * jnp.exp(rs - rtop), axis=1, keepdims=True)
    rlse = rtop + jnp.log(jnp.where(rsum > 0, rsum, 1.0))

    for copy in sent:
        copy.wait_send()
    pool_all.wait_send()
    z_all(gz, gz_s, gz_r).wait_send()
    z_all(qb.at[y], qz_s, qz_r).wait_send()
    y_all(ym, ym_s, ym_r).wait_send()
    y_all(gb, gy_s, gy_r).wait_send()

    z_all(lz, lz_s, lz_r).wait_recv()
    count = cm[...]
    own = jnp.where(count > 0, lz[...].reshape(128, 128), NEG)
    top = jnp.max(own, axis=0, keepdims=True)
    weight = count * jnp.exp(own - top)
    total = jnp.sum(weight, axis=0, keepdims=True)
    alse = top + jnp.log(jnp.where(total > 0, total, 1.0))
    row = lax.broadcasted_iota(jnp.int32, (8, 128), 0)
    yb[y] = jnp.where(row == 4, jnp.broadcast_to(alse, (8, 128)), jnp.broadcast_to(rlse, (8, 128)))
    y_send(yb, yb_s, yb_r)
    w1, w2 = split2(weight)
    lane = lax.broadcasted_iota(jnp.int32, (8, 128), 1)
    group = jnp.where(lax.rem(lane // answers, Y) == row, 1.0 / (answers * total_heads), 0.0)
    z_all(lz, lz_s, lz_r).wait_send()
    z_all(pgz, pg_s, pg_r).wait_send()
    core_copy.wait_send()
    y_all(qb, qw_s, qw_r).wait()
    y_all(yb, yb_s, yb_r).wait_recv()
    parts = yb[...]
    ptop = jnp.max(parts, axis=0)
    whole = ptop + jnp.log(jnp.sum(jnp.exp(parts - ptop[None]), axis=0))
    g1, g2 = split2(group * jnp.exp(top - whole[4:5, :]))
    mb[m] = dot_nt(g1, w1) + dot_nt(g1, w2) + dot_nt(g2, w1)

    def mb_copy(i):
        return remote(mb.at[m], mb.at[m], mb_s, mb_r, (d, lax.rem(m + i, M8)))

    mb_all = remote(mb.at[pl.ds(0, M8 - 1)], mb.at[pl.ds(0, M8 - 1)], mb_s, mb_r, (d, sib))
    for i in range(1, M8):
        mb_copy(i).start()
    probs = count4 * jnp.exp(rs - whole)

    def spread_embed(s, carry):
        qx[s] = jnp.zeros((8, dr), F32)
        for i in range(Y):
            for j in range(nb):
                qx[s, i:i + 1, j * 128:(j + 1) * 128] = qb[i, s, j:j + 1, :]
        return carry

    lax.fori_loop(0, Z, spread_embed, 0)
    embed_all = qx[...].reshape(Z * 8, dr).astype(BF16)
    mine_only = jnp.where(lane == row + z * p_dev, 1.0, 0.0).astype(BF16)
    y_all(yb, yb_s, yb_r).wait_send()
    mb_all.wait_recv()
    delta = probs - jnp.sum(mb[...], axis=0)
    dz[z] = delta
    z_send(dz, dz_s, dz_r)
    d1, d2 = split2(delta)
    grads = dot(d1, em[0]) + dot(d1, em[1]) + dot(d2, em[0])
    for i in range(Y):
        gs[i] = grads[i:i + 1, :]

    def qy_copy(i):
        to = lax.rem(y + i, Y)
        return remote(gs.at[to], gyr.at[y], qy_s, qy_r, (to * Z + z, m))

    for i in range(1, Y):
        qy_copy(i).start()
    gyr[y] = gs[y]
    mb_all.wait_send()
    y_all(gyr, qy_s, qy_r).wait()
    gq_out[...] = gyr[0] + gyr[1] + gyr[2] + gyr[3]
    z_all(dz, dz_s, dz_r).wait()
    b1, b2 = [dot_nt(mine_only, part).astype(BF16) for part in split2(dz[...].reshape(Z * 8, 128))]
    ge_out[...] = dot(b1, embed_all) + dot(b2, embed_all)


def body(picks, query_embed, dec_queries, passage_states, retr_states, key_weight, retr_weight):
    dp = lax.axis_size("dp")
    mp = lax.axis_size("mp")
    Z = dp // Y
    p_dev, length, width = passage_states.shape
    answers, all_cols = dec_queries.shape[1:]
    dr = retr_weight.shape[0]
    rows = p_dev * length
    states = passage_states.reshape(rows, width)
    dec = dec_queries.reshape(answers, all_cols)
    half_rows = (dr // 256) * p_dev
    dma = pltpu.SemaphoreType.DMA
    vmem = pl.BlockSpec(memory_space=pltpu.VMEM)
    hbm = pl.BlockSpec(memory_space=pltpu.HBM)
    ge, gq = pl.pallas_call(
        functools.partial(kernel, Z, length, all_cols // HD),
        out_shape=(
            jax.ShapeDtypeStruct((p_dev, dr), F32),
            jax.ShapeDtypeStruct((1, dr), F32),
        ),
        in_specs=[hbm] * 7,
        out_specs=(vmem, vmem),
        scratch_shapes=[
            pltpu.SMEM(picks.shape, jnp.int32),
            pltpu.VMEM(query_embed.shape, BF16),
            pltpu.VMEM(dec.shape, BF16),
            pltpu.VMEM(retr_states.shape, BF16),
            pltpu.VMEM((mp, rows, width), BF16),
            pltpu.VMEM(key_weight.shape, BF16),
            pltpu.VMEM((dr, dr), BF16),
            pltpu.VMEM((Y, Z, 16, 128), BF16),
            pltpu.VMEM((Y, Z, 8, 128), F32),
            pltpu.VMEM((Y, 16, 128), F32),
            pltpu.VMEM((2, half_rows, 128), F32),
            pltpu.VMEM((mp, half_rows, 128), F32),
            pltpu.VMEM((2, Z, 32, 128), BF16),
            pltpu.VMEM((Z, 8, dr), F32),
            pltpu.VMEM((8, dr), F32),
            pltpu.VMEM((8, 128), F32),
            pltpu.VMEM((128, 128), F32),
            pltpu.VMEM((2, 128, dr), BF16),
            pltpu.VMEM((Z, 8, 128), F32),
            pltpu.VMEM((Z, 8, 128), F32),
            pltpu.VMEM((Y, 8, 128), F32),
            pltpu.VMEM((mp, 8, 128), F32),
            pltpu.VMEM((Z, 8, 128), F32),
            pltpu.VMEM((Y, 1, dr), F32),
            pltpu.VMEM((Y, 1, dr), F32),
            dma((7,)),
            dma((28,)), dma((mp, CHUNKS)),
            *[dma] * 26,
        ],
        compiler_params=pltpu.CompilerParams(
            collective_id=0, has_side_effects=True, vmem_limit_bytes=63 * 1024 * 1024
        ),
    )(picks, query_embed, dec, states, retr_states, key_weight, retr_weight)
    return ge, gq


def solution(mesh):
    placed = (
        P("dp", None),
        P("dp", None),
        P("dp", None, None),
        P("dp", None, "mp"),
        P("dp", "mp", None),
        P(None, "mp"),
        P(),
    )
    return jax.shard_map(
        body, mesh=mesh, in_specs=placed, out_specs=(P("dp", None), P("dp", None)), check_vma=False
    )
```

```python
import functools

import jax
import jax.numpy as jnp
from jax import lax
from jax.experimental import pallas as pl
from jax.experimental.pallas import tpu as pltpu
from jax.sharding import PartitionSpec as P

HD = 64
MESH = pl.DeviceIdType.MESH
NEG = -3e38
F32 = jnp.float32
BF16 = jnp.bfloat16
NT = (((1,), (1,)), ((), ()))
CHUNKS = 4
Y = 4
X = 4


def dot(a, b):
    return jnp.dot(a, b, preferred_element_type=F32)


def dot_nt(a, b):
    return lax.dot_general(a, b, NT, preferred_element_type=F32)


def split2(a):
    first = a.astype(BF16)
    return first, (a - first.astype(F32)).astype(BF16)


def kernel(
    Z, length, total_heads,
    picks_hbm, qe_hbm, dec_hbm, states, retr_hbm, kw, rw,
    ge_out, gq_out,
    picks, qe, dec, retr, st, wb, wrb, gb, qb, ym, pp, pr, pg, qx, q8, c4, cm, em, ob, lz, yb, mb, dz, dp_all, gs, gyr,
    load_sem, st_s, st_r, gz_s, gz_r, gy_s, gy_r, qz_s, qz_r, qw_s, qw_r, ym_s, ym_r, pr_s, pr_r, pg_s, pg_r,
    pc_s, pc_r, lz_s, lz_r, yb_s, yb_r, mb_s, mb_r, dz_s, dz_r, qy_s, qy_r,
):
    d = lax.axis_index("dp")
    m = lax.axis_index("mp")
    y, z = d // Z, lax.rem(d, Z)
    x, c = m // 2, lax.rem(m, 2)
    M8 = 2 * X
    other = 1 - c
    xl, xr, xo = lax.rem(x + X - 1, X), lax.rem(x + 1, X), lax.rem(x + 2, X)
    mL, mR, mO, sib = xl * 2 + c, xr * 2 + c, xo * 2 + c, x * 2 + other
    sL, sR, sO = xl * 2 + other, xr * 2 + other, xo * 2 + other
    rows, width = states.shape
    step = rows // CHUNKS
    answers = dec.shape[0]
    p_dev = rows // length
    dr = qe.shape[1]
    nb = dr // 128
    half = nb // 2

    load_st = pltpu.make_async_copy(states, st.at[m], load_sem.at[0])
    load_w = pltpu.make_async_copy(kw, wb, load_sem.at[1])
    load_r = pltpu.make_async_copy(rw, wrb, load_sem.at[2])
    load_dec = pltpu.make_async_copy(dec_hbm, dec, load_sem.at[3])
    load_qe = pltpu.make_async_copy(qe_hbm, qe, load_sem.at[4])
    load_picks = pltpu.make_async_copy(picks_hbm, picks, load_sem.at[5])
    load_retr = pltpu.make_async_copy(retr_hbm, retr, load_sem.at[6])
    for copy in (load_dec, load_qe, load_picks, load_retr, load_st, load_w, load_r):
        copy.start()

    barrier = pltpu.get_barrier_semaphore()

    def far_first(act):
        def two(i, carry):
            act(lax.rem(z + Z // 2 + i, Z))
            act(lax.rem(z + Z // 2 - 1 - i, Z))
            return carry

        lax.fori_loop(0, Z // 2 - 1, two, 0)
        act(lax.rem(z + Z - 1, Z))

    def hello(zt):
        pl.semaphore_signal(barrier, inc=1, device_id=(y * Z + zt, m), device_id_type=MESH)

    far_first(hello)
    for i in range(1, Y):
        pl.semaphore_signal(barrier, inc=1, device_id=(lax.rem(y + i, Y) * Z + z, m), device_id_type=MESH)
    for i in range(1, M8):
        pl.semaphore_signal(barrier, inc=1, device_id=(d, lax.rem(m + i, M8)), device_id_type=MESH)

    pl.semaphore_wait(barrier, Z - 1 + Y - 1 + M8 - 1)
    def remote(src, dst, ssem, rsem, dev):
        return pltpu.make_async_remote_copy(src, dst, ssem, rsem, device_id=dev, device_id_type=MESH)

    def z_send(buf, ssem, rsem):
        far_first(lambda zt: remote(buf.at[z], buf.at[z], ssem, rsem, (y * Z + zt, m)).start())

    def z_all(buf, ssem, rsem):
        at = buf.at[pl.ds(0, Z - 1)]
        return remote(at, at, ssem, rsem, (y * Z + lax.rem(z + 1, Z), m))

    def y_copy(buf, ssem, rsem, i):
        to = lax.rem(y + i, Y) * Z + z
        return remote(buf.at[y], buf.at[y], ssem, rsem, (to, m))

    def y_all(buf, ssem, rsem):
        at = buf.at[pl.ds(0, Y - 1)]
        return remote(at, at, ssem, rsem, (lax.rem(y + 1, Y) * Z + z, m))

    def y_send(buf, ssem, rsem):
        for i in range(1, Y):
            y_copy(buf, ssem, rsem, i).start()

    sent = []

    def push(src, j, to, own=False):
        k = len(sent)
        at = st.at[src, pl.ds(j * step, step), :]
        copy = remote(states.at[pl.ds(j * step, step), :] if own else at, at, st_s.at[k], st_r.at[src, j], (d, to))
        copy.start()
        sent.append(copy)

    def arrived(src, j):
        at = st.at[src, pl.ds(j * step, step), :]
        remote(at, at, st_s.at[0], st_r.at[src, j], (d, sib)).wait_recv()

    gz = gb.at[y]
    h2 = CHUNKS // 2
    for i in range(h2):
        push(m, i, mR, True)
        push(m, i + h2, mL, True)

    load_dec.wait()
    mine = dec[:, pl.ds(pl.multiple_of(m * 256, 256), 256)].astype(F32)
    gb[y, z] = jnp.concatenate([mine[:, :128], mine[:, 128:]], axis=0).astype(BF16)
    z_send(gz, gz_s, gz_r)

    load_retr.wait()
    part = jnp.sum(retr[...].astype(F32), axis=1)
    for h in range(2):
        for j in range(half):
            b = h * half + j
            pp[h, j * p_dev:(j + 1) * p_dev, :] = part[:, b * 128:(b + 1) * 128]

    def pool_copy(i):
        to = lax.rem(m + i, M8)
        return remote(pp.at[lax.rem(to, 2)], pr.at[m], pr_s, pr_r, (d, to))

    for i in range(1, M8):
        pool_copy(i).start()

    for i in range(h2):
        push(m, i + h2, mR, True)
        push(m, i, mL, True)
    for i in range(CHUNKS):
        push(m, i, sib, True)

    def product(src):
        return dot(st[src], wb[pl.ds(pl.multiple_of(src * width, width), width), :])

    for j in range(h2):
        arrived(mL, j)
        push(mL, j, mR)
        push(mL, j, sib)
        arrived(mR, j + h2)
        push(mR, j + h2, mL)
        push(mR, j + h2, sib)

    load_picks.wait()
    load_qe.wait()
    ident = lax.broadcasted_iota(jnp.int32, (8, 128), 0) * 128 + lax.broadcasted_iota(jnp.int32, (8, 128), 1)
    counts = jnp.zeros((8, 128), F32)
    for k in range(picks.shape[1]):
        counts = counts + jnp.where(ident == picks[0, k], 1.0, 0.0)
    ym[y, 0:8, :] = jnp.zeros((8, 128), F32)
    qf = qe[...].astype(F32)
    for j in range(nb):
        ym[y, j:j + 1, :] = qf[:, j * 128:(j + 1) * 128]
    ym[y, 8:16, :] = counts
    qb[y, z] = ym[y, 0:8, :]
    y_send(ym, ym_s, ym_r)
    z_send(qb.at[y], qz_s, qz_r)

    pool_all = remote(pr.at[pl.ds(0, M8 - 1)], pr.at[pl.ds(0, M8 - 1)], pr_s, pr_r, (d, sib))
    pool_all.wait_recv()
    pooled = pp[c]
    for i in range(1, M8):
        pooled = pooled + pr[lax.rem(m + i, M8)]
    pooled = pooled / length
    pg[c, z] = jnp.concatenate([pooled, jnp.zeros((32 - half * p_dev, 128), F32)], axis=0).astype(BF16)
    z_send(pg.at[c], pg_s, pg_r)

    load_st.wait()
    load_w.wait()

    keys = product(m)

    for j in range(h2):
        arrived(mL, j + h2)
        push(mL, j + h2, sib)
        arrived(mR, j)
        push(mR, j, sib)

    z_all(gz, gz_s, gz_r).wait_recv()
    y_send(gb, gy_s, gy_r)

    for j in range(CHUNKS):
        arrived(sib, j)
    keys = keys + product(mL) + product(mR) + product(sib)
    for j in range(h2):
        arrived(mO, j)
        push(mO, j, sib)
        arrived(mO, j + h2)
        push(mO, j + h2, sib)
    keys = keys + product(mO)
    for src in (sL, sR, sO):
        for j in range(CHUNKS):
            arrived(src, j)
        keys = keys + product(src)

    to_row = lax.broadcasted_iota(jnp.int32, (rows, rows), 0)
    from_row = lax.broadcasted_iota(jnp.int32, (rows, rows), 1)
    perm = jnp.where(
        from_row == lax.rem(to_row, p_dev) * length + to_row // p_dev, 1.0, 0.0
    ).astype(BF16)
    k1, k2 = [dot(perm, k).astype(BF16) for k in split2(keys)]

    y_all(gb, gy_s, gy_r).wait_recv()
    low = lax.broadcasted_iota(jnp.int32, (8, 128), 1) < HD
    zero = jnp.zeros((8, 128), F32)
    zeros = jnp.zeros((64, 128), F32)

    def spread_queries(s):
        got = [gb[i, s].astype(F32) for i in range(Y)]
        left = [jnp.where(low, g[0:8], zero) for g in got] + [jnp.where(low, zero, g[0:8]) for g in got]
        right = [jnp.where(low, g[8:16], zero) for g in got] + [jnp.where(low, zero, g[8:16]) for g in got]
        left = jnp.concatenate(left + [zeros], axis=0)
        right = jnp.concatenate([zeros] + right, axis=0)
        return jnp.concatenate([left, right], axis=1).astype(BF16)

    def lz_copy(zt):
        return remote(ob.at[zt], lz.at[z], lz_s, lz_r, (y * Z + zt, m))

    def lse_pair(z0, z1):
        both = jnp.concatenate([spread_queries(z0), spread_queries(z1)], axis=0)
        scores = dot_nt(k1, both) + dot_nt(k2, both)
        scores = scores.reshape(length, p_dev, 256)
        top = jnp.max(scores, axis=0)
        return top + jnp.log(jnp.sum(jnp.exp(scores - top[None]), axis=0))

    def far_near(i):
        return lax.rem(z + Z // 2 + i, Z), lax.rem(z + Z // 2 - 1 - i, Z)

    def score_step(i, carry):
        z0, z1 = far_near(i)
        lse = lse_pair(z0, z1)
        ob[z0] = lse[:, :128]
        ob[z1] = lse[:, 128:]
        lz_copy(z0).start()
        lz_copy(z1).start()
        return carry

    lax.fori_loop(0, Z // 2 - 1, score_step, 0)
    zlast, _ = far_near(Z // 2 - 1)
    lse = lse_pair(zlast, z)
    ob[zlast] = lse[:, :128]
    lz_copy(zlast).start()
    lz[z] = lse[:, 128:]

    y_all(ym, ym_s, ym_r).wait_recv()
    q8[...] = jnp.zeros_like(q8)
    c4[...] = jnp.zeros_like(c4)
    for i in range(Y):
        c4[i:i + 1, :] = ym[i, pl.ds(8 + y, 1), :]
        for j in range(nb):
            q8[i:i + 1, j * 128:(j + 1) * 128] = ym[i, j:j + 1, :]
    spread = jnp.concatenate(
        [jnp.broadcast_to(c4[i:i + 1, :], (answers, 128)) for _ in range(128 // (Y * answers)) for i in range(Y)], axis=0
    )
    cm[...] = spread.T

    z_all(qb.at[y], qz_s, qz_r).wait_recv()
    y_send(qb, qw_s, qw_r)

    pgz = pg.at[c]
    z_all(pgz, pg_s, pg_r).wait_recv()
    core_copy = remote(pg.at[c], pg.at[c], pc_s, pc_r, (d, sib))
    core_copy.start()
    load_r.wait()
    remote(pg.at[other], pg.at[other], pc_s, pc_r, (d, sib)).wait_recv()
    embeds = None
    for h in range(2):
        got = pg[h].astype(F32)
        for j in range(half):
            b = h * half + j
            piece = got[:, j * p_dev:(j + 1) * p_dev, :].reshape(Z * p_dev, 128).astype(BF16)
            term = dot(piece, wrb[b * 128:(b + 1) * 128, :])
            embeds = term if embeds is None else embeds + term
    e1, e2 = split2(embeds)
    em[0] = e1
    em[1] = e2
    count4 = c4[...]
    q1 = q8[...].astype(BF16)
    rs = dot_nt(q1, e1) + dot_nt(q1, e2) + dot_nt(q1, (embeds - e1.astype(F32) - e2.astype(F32)).astype(BF16))
    rs = jnp.where(count4 > 0, rs, NEG)
    rtop = jnp.max(rs, axis=1, keepdims=True)
    rsum = jnp.sum(count4 * jnp.exp(rs - rtop), axis=1, keepdims=True)
    rlse = rtop + jnp.log(jnp.where(rsum > 0, rsum, 1.0))

    for copy in sent:
        copy.wait_send()
    pool_all.wait_send()
    z_all(gz, gz_s, gz_r).wait_send()
    z_all(qb.at[y], qz_s, qz_r).wait_send()
    y_all(ym, ym_s, ym_r).wait_send()
    y_all(gb, gy_s, gy_r).wait_send()

    z_all(lz, lz_s, lz_r).wait_recv()
    count = cm[...]
    own = jnp.where(count > 0, lz[...].reshape(128, 128), NEG)
    top = jnp.max(own, axis=0, keepdims=True)
    weight = count * jnp.exp(own - top)
    total = jnp.sum(weight, axis=0, keepdims=True)
    alse = top + jnp.log(jnp.where(total > 0, total, 1.0))
    row = lax.broadcasted_iota(jnp.int32, (8, 128), 0)
    yb[y] = jnp.where(row == 4, jnp.broadcast_to(alse, (8, 128)), jnp.broadcast_to(rlse, (8, 128)))
    y_send(yb, yb_s, yb_r)
    w1, w2 = split2(weight)
    lane = lax.broadcasted_iota(jnp.int32, (8, 128), 1)
    group = jnp.where(lax.rem(lane // answers, Y) == row, 1.0 / (answers * total_heads), 0.0)
    z_all(lz, lz_s, lz_r).wait_send()
    z_all(pgz, pg_s, pg_r).wait_send()
    core_copy.wait_send()
    y_all(qb, qw_s, qw_r).wait()
    y_all(yb, yb_s, yb_r).wait_recv()
    parts = yb[...]
    ptop = jnp.max(parts, axis=0)
    whole = ptop + jnp.log(jnp.sum(jnp.exp(parts - ptop[None]), axis=0))
    g1, g2 = split2(group * jnp.exp(top - whole[4:5, :]))
    mb[m] = dot_nt(g1, w1) + dot_nt(g1, w2) + dot_nt(g2, w1)

    def mb_copy(i):
        return remote(mb.at[m], mb.at[m], mb_s, mb_r, (d, lax.rem(m + i, M8)))

    mb_all = remote(mb.at[pl.ds(0, M8 - 1)], mb.at[pl.ds(0, M8 - 1)], mb_s, mb_r, (d, sib))
    for i in range(1, M8):
        mb_copy(i).start()
    probs = count4 * jnp.exp(rs - whole)

    def spread_embed(s, carry):
        qx[s] = jnp.zeros((8, dr), F32)
        for i in range(Y):
            for j in range(nb):
                qx[s, i:i + 1, j * 128:(j + 1) * 128] = qb[i, s, j:j + 1, :]
        return carry

    lax.fori_loop(0, Z, spread_embed, 0)
    embed_all = qx[...].reshape(Z * 8, dr).astype(BF16)
    mine_only = jnp.where(lane == row + z * p_dev, 1.0, 0.0).astype(BF16)
    dp_all[...] = jnp.zeros_like(dp_all)
    y_all(yb, yb_s, yb_r).wait_send()
    mb_all.wait_recv()
    delta = probs - jnp.sum(mb[...], axis=0)
    dz[z] = delta[:Y]
    z_send(dz, dz_s, dz_r)
    d1, d2 = split2(delta)
    grads = dot(d1, em[0]) + dot(d1, em[1]) + dot(d2, em[0])
    for i in range(Y):
        gs[i] = grads[i:i + 1, :]

    def qy_copy(i):
        to = lax.rem(y + i, Y)
        return remote(gs.at[to], gyr.at[y], qy_s, qy_r, (to * Z + z, m))

    for i in range(1, Y):
        qy_copy(i).start()
    gyr[y] = gs[y]
    mb_all.wait_send()
    y_all(gyr, qy_s, qy_r).wait()
    gq_out[...] = gyr[0] + gyr[1] + gyr[2] + gyr[3]
    z_all(dz, dz_s, dz_r).wait()
    for i in range(Z):
        dp_all[i * 8:i * 8 + Y, :] = dz[i]
    b1, b2 = [dot_nt(mine_only, part).astype(BF16) for part in split2(dp_all[...])]
    ge_out[...] = dot(b1, embed_all) + dot(b2, embed_all)


def body(picks, query_embed, dec_queries, passage_states, retr_states, key_weight, retr_weight):
    dp = lax.axis_size("dp")
    mp = lax.axis_size("mp")
    Z = dp // Y
    p_dev, length, width = passage_states.shape
    answers, all_cols = dec_queries.shape[1:]
    dr = retr_weight.shape[0]
    rows = p_dev * length
    states = passage_states.reshape(rows, width)
    dec = dec_queries.reshape(answers, all_cols)
    half_rows = (dr // 256) * p_dev
    dma = pltpu.SemaphoreType.DMA
    vmem = pl.BlockSpec(memory_space=pltpu.VMEM)
    hbm = pl.BlockSpec(memory_space=pltpu.HBM)
    ge, gq = pl.pallas_call(
        functools.partial(kernel, Z, length, all_cols // HD),
        out_shape=(
            jax.ShapeDtypeStruct((p_dev, dr), F32),
            jax.ShapeDtypeStruct((1, dr), F32),
        ),
        in_specs=[hbm] * 7,
        out_specs=(vmem, vmem),
        scratch_shapes=[
            pltpu.SMEM(picks.shape, jnp.int32),
            pltpu.VMEM(query_embed.shape, BF16),
            pltpu.VMEM(dec.shape, BF16),
            pltpu.VMEM(retr_states.shape, BF16),
            pltpu.VMEM((mp, rows, width), BF16),
            pltpu.VMEM(key_weight.shape, BF16),
            pltpu.VMEM((dr, dr), BF16),
            pltpu.VMEM((Y, Z, 16, 128), BF16),
            pltpu.VMEM((Y, Z, 8, 128), F32),
            pltpu.VMEM((Y, 16, 128), F32),
            pltpu.VMEM((2, half_rows, 128), F32),
            pltpu.VMEM((mp, half_rows, 128), F32),
            pltpu.VMEM((2, Z, 32, 128), BF16),
            pltpu.VMEM((Z, 8, dr), F32),
            pltpu.VMEM((8, dr), F32),
            pltpu.VMEM((8, 128), F32),
            pltpu.VMEM((128, 128), F32),
            pltpu.VMEM((2, 128, dr), BF16),
            pltpu.VMEM((Z, 8, 128), F32),
            pltpu.VMEM((Z, 8, 128), F32),
            pltpu.VMEM((Y, 8, 128), F32),
            pltpu.VMEM((mp, 8, 128), F32),
            pltpu.VMEM((Z, Y, 128), F32),
            pltpu.VMEM((Z * 8, 128), F32),
            pltpu.VMEM((Y, 1, dr), F32),
            pltpu.VMEM((Y, 1, dr), F32),
            dma((7,)),
            dma((7 * CHUNKS,)), dma((mp, CHUNKS)),
            *[dma] * 26,
        ],
        compiler_params=pltpu.CompilerParams(
            collective_id=0, has_side_effects=True, vmem_limit_bytes=63 * 1024 * 1024
        ),
    )(picks, query_embed, dec, states, retr_states, key_weight, retr_weight)
    return ge, gq


def solution(mesh):
    placed = (
        P("dp", None),
        P("dp", None),
        P("dp", None, None),
        P("dp", None, "mp"),
        P("dp", "mp", None),
        P(None, "mp"),
        P(),
    )
    return jax.shard_map(
        body, mesh=mesh, in_specs=placed, out_specs=(P("dp", None), P("dp", None)), check_vma=False
    )
```

```python
import functools

import jax
import jax.numpy as jnp
from jax import lax
from jax.experimental import pallas as pl
from jax.experimental.pallas import tpu as pltpu
from jax.sharding import PartitionSpec as P

HD = 64
MESH = pl.DeviceIdType.MESH
NEG = -3e38
F32 = jnp.float32
BF16 = jnp.bfloat16
NT = (((1,), (1,)), ((), ()))
CHUNKS = 2
Y = 4
X = 4


def dot(a, b):
    return jnp.dot(a, b, preferred_element_type=F32)


def dot_nt(a, b):
    return lax.dot_general(a, b, NT, preferred_element_type=F32)


def split2(a):
    first = a.astype(BF16)
    return first, (a - first.astype(F32)).astype(BF16)


def kernel(
    Z, length, total_heads,
    picks_hbm, qe_hbm, dec_hbm, states, retr_hbm, kw, rw,
    ge_out, gq_out,
    picks, qe, dec, retr, st, wb, wrb, gb, qb, ym, pp, pr, pg, qx, q8, c4, cm, em, ob, lz, yb, mb, dz, dp_all, gs, gyr,
    load_sem, st_s, st_r, gz_s, gz_r, gy_s, gy_r, qz_s, qz_r, qw_s, qw_r, ym_s, ym_r, pr_s, pr_r, pg_s, pg_r,
    pc_s, pc_r, lz_s, lz_r, yb_s, yb_r, mb_s, mb_r, dz_s, dz_r, qy_s, qy_r,
):
    d = lax.axis_index("dp")
    m = lax.axis_index("mp")
    y, z = d // Z, lax.rem(d, Z)
    x, c = m // 2, lax.rem(m, 2)
    M8 = 2 * X
    other = 1 - c
    xl, xr, xo = lax.rem(x + X - 1, X), lax.rem(x + 1, X), lax.rem(x + 2, X)
    mL, mR, mO, sib = xl * 2 + c, xr * 2 + c, xo * 2 + c, x * 2 + other
    sL, sR, sO = xl * 2 + other, xr * 2 + other, xo * 2 + other
    rows, width = states.shape
    step = rows // CHUNKS
    answers = dec.shape[0]
    p_dev = rows // length
    dr = qe.shape[1]
    nb = dr // 128
    half = nb // 2

    load_st = pltpu.make_async_copy(states, st.at[m], load_sem.at[0])
    load_w = pltpu.make_async_copy(kw, wb, load_sem.at[1])
    load_r = pltpu.make_async_copy(rw, wrb, load_sem.at[2])
    load_dec = pltpu.make_async_copy(dec_hbm, dec, load_sem.at[3])
    load_qe = pltpu.make_async_copy(qe_hbm, qe, load_sem.at[4])
    load_picks = pltpu.make_async_copy(picks_hbm, picks, load_sem.at[5])
    load_retr = pltpu.make_async_copy(retr_hbm, retr, load_sem.at[6])
    for copy in (load_dec, load_qe, load_picks, load_retr, load_st, load_w, load_r):
        copy.start()

    barrier = pltpu.get_barrier_semaphore()

    def far_first(act):
        def two(i, carry):
            act(lax.rem(z + Z // 2 + i, Z))
            act(lax.rem(z + Z // 2 - 1 - i, Z))
            return carry

        lax.fori_loop(0, Z // 2 - 1, two, 0)
        act(lax.rem(z + Z - 1, Z))

    def hello(zt):
        pl.semaphore_signal(barrier, inc=1, device_id=(y * Z + zt, m), device_id_type=MESH)

    far_first(hello)
    for i in range(1, Y):
        pl.semaphore_signal(barrier, inc=1, device_id=(lax.rem(y + i, Y) * Z + z, m), device_id_type=MESH)
    for i in range(1, M8):
        pl.semaphore_signal(barrier, inc=1, device_id=(d, lax.rem(m + i, M8)), device_id_type=MESH)

    pl.semaphore_wait(barrier, Z - 1 + Y - 1 + M8 - 1)
    def remote(src, dst, ssem, rsem, dev):
        return pltpu.make_async_remote_copy(src, dst, ssem, rsem, device_id=dev, device_id_type=MESH)

    def z_send(buf, ssem, rsem):
        far_first(lambda zt: remote(buf.at[z], buf.at[z], ssem, rsem, (y * Z + zt, m)).start())

    def z_all(buf, ssem, rsem):
        at = buf.at[pl.ds(0, Z - 1)]
        return remote(at, at, ssem, rsem, (y * Z + lax.rem(z + 1, Z), m))

    def y_copy(buf, ssem, rsem, i):
        to = lax.rem(y + i, Y) * Z + z
        return remote(buf.at[y], buf.at[y], ssem, rsem, (to, m))

    def y_all(buf, ssem, rsem):
        at = buf.at[pl.ds(0, Y - 1)]
        return remote(at, at, ssem, rsem, (lax.rem(y + 1, Y) * Z + z, m))

    def y_send(buf, ssem, rsem):
        for i in range(1, Y):
            y_copy(buf, ssem, rsem, i).start()

    sent = []

    def push(src, j, to, own=False):
        k = len(sent)
        at = st.at[src, pl.ds(j * step, step), :]
        copy = remote(states.at[pl.ds(j * step, step), :] if own else at, at, st_s.at[k], st_r.at[src, j], (d, to))
        copy.start()
        sent.append(copy)

    def arrived(src, j):
        at = st.at[src, pl.ds(j * step, step), :]
        remote(at, at, st_s.at[0], st_r.at[src, j], (d, sib)).wait_recv()

    gz = gb.at[y]
    h2 = CHUNKS // 2
    for i in range(h2):
        push(m, i, mR, True)
        push(m, i + h2, mL, True)

    load_dec.wait()
    mine = dec[:, pl.ds(pl.multiple_of(m * 256, 256), 256)].astype(F32)
    gb[y, z] = jnp.concatenate([mine[:, :128], mine[:, 128:]], axis=0).astype(BF16)
    z_send(gz, gz_s, gz_r)

    load_retr.wait()
    part = jnp.sum(retr[...].astype(F32), axis=1)
    for h in range(2):
        for j in range(half):
            b = h * half + j
            pp[h, j * p_dev:(j + 1) * p_dev, :] = part[:, b * 128:(b + 1) * 128]

    def pool_copy(i):
        to = lax.rem(m + i, M8)
        return remote(pp.at[lax.rem(to, 2)], pr.at[m], pr_s, pr_r, (d, to))

    for i in range(1, M8):
        pool_copy(i).start()

    for i in range(h2):
        push(m, i + h2, mR, True)
        push(m, i, mL, True)
    for i in range(CHUNKS):
        push(m, i, sib, True)

    def product(src):
        return dot(st[src], wb[pl.ds(pl.multiple_of(src * width, width), width), :])

    for j in range(h2):
        arrived(mL, j)
        push(mL, j, mR)
        push(mL, j, sib)
        arrived(mR, j + h2)
        push(mR, j + h2, mL)
        push(mR, j + h2, sib)

    load_picks.wait()
    load_qe.wait()
    ident = lax.broadcasted_iota(jnp.int32, (8, 128), 0) * 128 + lax.broadcasted_iota(jnp.int32, (8, 128), 1)
    counts = jnp.zeros((8, 128), F32)
    for k in range(picks.shape[1]):
        counts = counts + jnp.where(ident == picks[0, k], 1.0, 0.0)
    ym[y, 0:8, :] = jnp.zeros((8, 128), F32)
    qf = qe[...].astype(F32)
    for j in range(nb):
        ym[y, j:j + 1, :] = qf[:, j * 128:(j + 1) * 128]
    ym[y, 8:16, :] = counts
    qb[y, z] = ym[y, 0:8, :]
    y_send(ym, ym_s, ym_r)
    z_send(qb.at[y], qz_s, qz_r)

    pool_all = remote(pr.at[pl.ds(0, M8 - 1)], pr.at[pl.ds(0, M8 - 1)], pr_s, pr_r, (d, sib))
    pool_all.wait_recv()
    pooled = pp[c]
    for i in range(1, M8):
        pooled = pooled + pr[lax.rem(m + i, M8)]
    pooled = pooled / length
    pg[c, z] = jnp.concatenate([pooled, jnp.zeros((32 - half * p_dev, 128), F32)], axis=0).astype(BF16)
    z_send(pg.at[c], pg_s, pg_r)

    load_st.wait()
    load_w.wait()

    keys = product(m)

    for j in range(h2):
        arrived(mL, j + h2)
        push(mL, j + h2, sib)
        arrived(mR, j)
        push(mR, j, sib)

    z_all(gz, gz_s, gz_r).wait_recv()
    y_send(gb, gy_s, gy_r)

    for j in range(CHUNKS):
        arrived(sib, j)
    keys = keys + product(mL) + product(mR) + product(sib)
    for j in range(h2):
        arrived(mO, j)
        push(mO, j, sib)
        arrived(mO, j + h2)
        push(mO, j + h2, sib)
    keys = keys + product(mO)
    for src in (sL, sR, sO):
        for j in range(CHUNKS):
            arrived(src, j)
        keys = keys + product(src)

    to_row = lax.broadcasted_iota(jnp.int32, (rows, rows), 0)
    from_row = lax.broadcasted_iota(jnp.int32, (rows, rows), 1)
    perm = jnp.where(
        from_row == lax.rem(to_row, p_dev) * length + to_row // p_dev, 1.0, 0.0
    ).astype(BF16)
    k1, k2 = [dot(perm, k).astype(BF16) for k in split2(keys)]

    y_all(gb, gy_s, gy_r).wait_recv()
    low = lax.broadcasted_iota(jnp.int32, (8, 128), 1) < HD
    zero = jnp.zeros((8, 128), F32)
    zeros = jnp.zeros((64, 128), F32)

    def spread_queries(s):
        got = [gb[i, s].astype(F32) for i in range(Y)]
        left = [jnp.where(low, g[0:8], zero) for g in got] + [jnp.where(low, zero, g[0:8]) for g in got]
        right = [jnp.where(low, g[8:16], zero) for g in got] + [jnp.where(low, zero, g[8:16]) for g in got]
        left = jnp.concatenate(left + [zeros], axis=0)
        right = jnp.concatenate([zeros] + right, axis=0)
        return jnp.concatenate([left, right], axis=1).astype(BF16)

    def lz_copy(zt):
        return remote(ob.at[zt], lz.at[z], lz_s, lz_r, (y * Z + zt, m))

    def lse_pair(z0, z1):
        both = jnp.concatenate([spread_queries(z0), spread_queries(z1)], axis=0)
        scores = dot_nt(k1, both) + dot_nt(k2, both)
        scores = scores.reshape(length, p_dev, 256)
        top = jnp.max(scores, axis=0)
        return top + jnp.log(jnp.sum(jnp.exp(scores - top[None]), axis=0))

    def far_near(i):
        return lax.rem(z + Z // 2 + i, Z), lax.rem(z + Z // 2 - 1 - i, Z)

    def score_step(i, carry):
        z0, z1 = far_near(i)
        lse = lse_pair(z0, z1)
        ob[z0] = lse[:, :128]
        ob[z1] = lse[:, 128:]
        lz_copy(z0).start()
        lz_copy(z1).start()
        return carry

    lax.fori_loop(0, Z // 2 - 1, score_step, 0)
    zlast, _ = far_near(Z // 2 - 1)
    lse = lse_pair(zlast, z)
    ob[zlast] = lse[:, :128]
    lz_copy(zlast).start()
    lz[z] = lse[:, 128:]

    y_all(ym, ym_s, ym_r).wait_recv()
    q8[...] = jnp.zeros_like(q8)
    c4[...] = jnp.zeros_like(c4)
    for i in range(Y):
        c4[i:i + 1, :] = ym[i, pl.ds(8 + y, 1), :]
        for j in range(nb):
            q8[i:i + 1, j * 128:(j + 1) * 128] = ym[i, j:j + 1, :]
    spread = jnp.concatenate(
        [jnp.broadcast_to(c4[i:i + 1, :], (answers, 128)) for _ in range(128 // (Y * answers)) for i in range(Y)], axis=0
    )
    cm[...] = spread.T

    z_all(qb.at[y], qz_s, qz_r).wait_recv()
    y_send(qb, qw_s, qw_r)

    pgz = pg.at[c]
    z_all(pgz, pg_s, pg_r).wait_recv()
    core_copy = remote(pg.at[c], pg.at[c], pc_s, pc_r, (d, sib))
    core_copy.start()
    load_r.wait()
    remote(pg.at[other], pg.at[other], pc_s, pc_r, (d, sib)).wait_recv()
    embeds = None
    for h in range(2):
        got = pg[h].astype(F32)
        for j in range(half):
            b = h * half + j
            piece = got[:, j * p_dev:(j + 1) * p_dev, :].reshape(Z * p_dev, 128).astype(BF16)
            term = dot(piece, wrb[b * 128:(b + 1) * 128, :])
            embeds = term if embeds is None else embeds + term
    e1, e2 = split2(embeds)
    em[0] = e1
    em[1] = e2
    count4 = c4[...]
    q1 = q8[...].astype(BF16)
    rs = dot_nt(q1, e1) + dot_nt(q1, e2) + dot_nt(q1, (embeds - e1.astype(F32) - e2.astype(F32)).astype(BF16))
    rs = jnp.where(count4 > 0, rs, NEG)
    rtop = jnp.max(rs, axis=1, keepdims=True)
    rsum = jnp.sum(count4 * jnp.exp(rs - rtop), axis=1, keepdims=True)
    rlse = rtop + jnp.log(jnp.where(rsum > 0, rsum, 1.0))

    for copy in sent:
        copy.wait_send()
    pool_all.wait_send()
    z_all(gz, gz_s, gz_r).wait_send()
    z_all(qb.at[y], qz_s, qz_r).wait_send()
    y_all(ym, ym_s, ym_r).wait_send()
    y_all(gb, gy_s, gy_r).wait_send()

    z_all(lz, lz_s, lz_r).wait_recv()
    count = cm[...]
    own = jnp.where(count > 0, lz[...].reshape(128, 128), NEG)
    top = jnp.max(own, axis=0, keepdims=True)
    weight = count * jnp.exp(own - top)
    total = jnp.sum(weight, axis=0, keepdims=True)
    alse = top + jnp.log(jnp.where(total > 0, total, 1.0))
    row = lax.broadcasted_iota(jnp.int32, (8, 128), 0)
    yb[y] = jnp.where(row == 4, jnp.broadcast_to(alse, (8, 128)), jnp.broadcast_to(rlse, (8, 128)))
    y_send(yb, yb_s, yb_r)
    w1, w2 = split2(weight)
    lane = lax.broadcasted_iota(jnp.int32, (8, 128), 1)
    group = jnp.where(lax.rem(lane // answers, Y) == row, 1.0 / (answers * total_heads), 0.0)
    z_all(lz, lz_s, lz_r).wait_send()
    z_all(pgz, pg_s, pg_r).wait_send()
    core_copy.wait_send()
    y_all(qb, qw_s, qw_r).wait()
    y_all(yb, yb_s, yb_r).wait_recv()
    parts = yb[...]
    ptop = jnp.max(parts, axis=0)
    whole = ptop + jnp.log(jnp.sum(jnp.exp(parts - ptop[None]), axis=0))
    g1, g2 = split2(group * jnp.exp(top - whole[4:5, :]))
    mb[m] = dot_nt(g1, w1) + dot_nt(g1, w2) + dot_nt(g2, w1)

    def mb_copy(i):
        return remote(mb.at[m], mb.at[m], mb_s, mb_r, (d, lax.rem(m + i, M8)))

    mb_all = remote(mb.at[pl.ds(0, M8 - 1)], mb.at[pl.ds(0, M8 - 1)], mb_s, mb_r, (d, sib))
    for i in range(1, M8):
        mb_copy(i).start()
    probs = count4 * jnp.exp(rs - whole)

    def spread_embed(s, carry):
        qx[s] = jnp.zeros((8, dr), F32)
        for i in range(Y):
            for j in range(nb):
                qx[s, i:i + 1, j * 128:(j + 1) * 128] = qb[i, s, j:j + 1, :]
        return carry

    lax.fori_loop(0, Z, spread_embed, 0)
    embed_all = qx[...].reshape(Z * 8, dr).astype(BF16)
    mine_only = jnp.where(lane == row + z * p_dev, 1.0, 0.0).astype(BF16)
    dp_all[...] = jnp.zeros_like(dp_all)
    y_all(yb, yb_s, yb_r).wait_send()
    mb_all.wait_recv()
    delta = probs - jnp.sum(mb[...], axis=0)
    dz[z] = delta[:Y]
    z_send(dz, dz_s, dz_r)
    d1, d2 = split2(delta)
    grads = dot(d1, em[0]) + dot(d1, em[1]) + dot(d2, em[0])
    for i in range(Y):
        gs[i] = grads[i:i + 1, :]

    def qy_copy(i):
        to = lax.rem(y + i, Y)
        return remote(gs.at[to], gyr.at[y], qy_s, qy_r, (to * Z + z, m))

    for i in range(1, Y):
        qy_copy(i).start()
    gyr[y] = gs[y]
    mb_all.wait_send()
    y_all(gyr, qy_s, qy_r).wait()
    gq_out[...] = gyr[0] + gyr[1] + gyr[2] + gyr[3]
    z_all(dz, dz_s, dz_r).wait()
    for i in range(Z):
        dp_all[i * 8:i * 8 + Y, :] = dz[i]
    b1, b2 = [dot_nt(mine_only, part).astype(BF16) for part in split2(dp_all[...])]
    ge_out[...] = dot(b1, embed_all) + dot(b2, embed_all)


def body(picks, query_embed, dec_queries, passage_states, retr_states, key_weight, retr_weight):
    dp = lax.axis_size("dp")
    mp = lax.axis_size("mp")
    Z = dp // Y
    p_dev, length, width = passage_states.shape
    answers, all_cols = dec_queries.shape[1:]
    dr = retr_weight.shape[0]
    rows = p_dev * length
    states = passage_states.reshape(rows, width)
    dec = dec_queries.reshape(answers, all_cols)
    half_rows = (dr // 256) * p_dev
    dma = pltpu.SemaphoreType.DMA
    vmem = pl.BlockSpec(memory_space=pltpu.VMEM)
    hbm = pl.BlockSpec(memory_space=pltpu.HBM)
    ge, gq = pl.pallas_call(
        functools.partial(kernel, Z, length, all_cols // HD),
        out_shape=(
            jax.ShapeDtypeStruct((p_dev, dr), F32),
            jax.ShapeDtypeStruct((1, dr), F32),
        ),
        in_specs=[hbm] * 7,
        out_specs=(vmem, vmem),
        scratch_shapes=[
            pltpu.SMEM(picks.shape, jnp.int32),
            pltpu.VMEM(query_embed.shape, BF16),
            pltpu.VMEM(dec.shape, BF16),
            pltpu.VMEM(retr_states.shape, BF16),
            pltpu.VMEM((mp, rows, width), BF16),
            pltpu.VMEM(key_weight.shape, BF16),
            pltpu.VMEM((dr, dr), BF16),
            pltpu.VMEM((Y, Z, 16, 128), BF16),
            pltpu.VMEM((Y, Z, 8, 128), F32),
            pltpu.VMEM((Y, 16, 128), F32),
            pltpu.VMEM((2, half_rows, 128), F32),
            pltpu.VMEM((mp, half_rows, 128), F32),
            pltpu.VMEM((2, Z, 32, 128), BF16),
            pltpu.VMEM((Z, 8, dr), F32),
            pltpu.VMEM((8, dr), F32),
            pltpu.VMEM((8, 128), F32),
            pltpu.VMEM((128, 128), F32),
            pltpu.VMEM((2, 128, dr), BF16),
            pltpu.VMEM((Z, 8, 128), F32),
            pltpu.VMEM((Z, 8, 128), F32),
            pltpu.VMEM((Y, 8, 128), F32),
            pltpu.VMEM((mp, 8, 128), F32),
            pltpu.VMEM((Z, Y, 128), F32),
            pltpu.VMEM((Z * 8, 128), F32),
            pltpu.VMEM((Y, 1, dr), F32),
            pltpu.VMEM((Y, 1, dr), F32),
            dma((7,)),
            dma((7 * CHUNKS,)), dma((mp, CHUNKS)),
            *[dma] * 26,
        ],
        compiler_params=pltpu.CompilerParams(
            collective_id=0, has_side_effects=True, vmem_limit_bytes=63 * 1024 * 1024
        ),
    )(picks, query_embed, dec, states, retr_states, key_weight, retr_weight)
    return ge, gq


def solution(mesh):
    placed = (
        P("dp", None),
        P("dp", None),
        P("dp", None, None),
        P("dp", None, "mp"),
        P("dp", "mp", None),
        P(None, "mp"),
        P(),
    )
    return jax.shard_map(
        body, mesh=mesh, in_specs=placed, out_specs=(P("dp", None), P("dp", None)), check_vma=False
    )
```
